256 devices in a mesh: cpx: 16 (over y, z_lo, core), cpy: 16 (over x, z_hi).
Axes of the slice: x: 4, y: 4, z: 8 (z_hi: 4, z_lo: 2; z = z_hi * 2 + z_lo), core: 2. Of those that a mesh axis runs over, the one named last changes fastest.
Arguments:
- queries: bfloat16 [49152, 1024], P(('cpx', 'cpy')), may hold values from -6 to 6
- grad_out: bfloat16 [49152, 1024], P(('cpx', 'cpy')), may hold values from -60 to 60
- attn_out: bfloat16 [49152, 1024], P(('cpx', 'cpy')), may hold values from -6 to 6
- saved_lse: float32 [8, 49152], P(None, ('cpx', 'cpy')), may hold values from 6 to 8
- key_rows: bfloat16 [196608, 128], P(('cpx', 'cpy')), may hold values from -6 to 6
- value_rows: bfloat16 [196608, 128], P(('cpx', 'cpy')), may hold values from -6 to 6
- doc_lengths: int32 [64], replicated, may hold values from 1 to 6144, 196608 in all
- read_steps: int32 [256, 4], replicated, may hold values from -1 to 255, as said below
Outputs:
- grad_queries: float32 [49152, 1024], P(('cpx', 'cpy'))
- grad_keys: float32 [196608, 128], P(('cpx', 'cpy'))
- grad_values: float32 [196608, 128], P(('cpx', 'cpy'))
The draws below stay inside these ranges and needn't reach their ends.
Inputs may be any that keep to these rules, and one draw needn't show every extreme that they name: `read_steps`: entry (d, t) is d - t if device d reads the key block of device d - t and -1 if not; entry (d, 0) is d; entries with d - t < 0 are -1.
All inputs are finite; a program needn't handle non-finite values.
Results may differ from the reference program's by a relative error of at most 0.0044.
Values may be sent and summed in bfloat16 or wider, within the bound.
No kernel may reach another device: no remote copies, remote signals or barrier semaphores. Data moves between devices by JAX's collectives and lax.ppermute only.
A program may use at most 64 MiB of HBM per device.

```python
import math
import jax
import jax.numpy as jnp
import numpy as np
from jax import lax

HEADS = 8
DH = 128
KB = 768
Q_DEV = 192
STEPS = 4
TOKENS = 49152
KEYS = 196608
NDOC = 64
DOC_MOST = 6144


def draw_read_steps(key, part):
    device_count = KEYS // KB
    readers = jnp.arange(device_count, dtype=jnp.int32)[:, None]
    distance = jnp.arange(STEPS, dtype=jnp.int32)[None, :]
    owners = readers - distance
    coin_draw = jax.random.randint(key, (device_count, STEPS), 0, 4)
    retained = ((coin_draw != 0) | (distance == 0)) & (owners >= 0)
    return jnp.where(retained, owners, -1).astype(jnp.int32)


def steps_of(key, dims, shards, smallest, largest):
    def one(axis_at, blocks):
        steps = jax.random.uniform(jax.random.fold_in(jax.random.fold_in(key, 6), axis_at), (blocks,), jnp.float32, smallest / len(shards), largest / len(shards))
        return jnp.repeat(jnp.exp(steps), dims[axis_at] // blocks).reshape((-1,) + (1,) * (len(dims) - axis_at - 1))

    level = one(*shards[0])
    for cut in shards[1:]:
        level = level * one(*cut)
    return level


def length_profile(number_of, total, bound, lean):
    loads = [(1 << 20) // math.isqrt(grade ** lean) + 1 for grade in range(2, number_of + 1)]
    rest, holding = total - bound - (number_of - 1), [1] * (number_of - 1)
    while rest > 0:
        candidates = [i for i in range(number_of - 1) if holding[i] < bound]
        pool, remaining = sum([loads[i] for i in candidates]), rest
        for i in candidates:
            addition = min(bound - holding[i], max(1, remaining * loads[i] // pool), rest)
            holding[i] = holding[i] + addition
            rest = rest - addition
    return np.array([bound] + holding)


def ragged_sizes(rng, number_of, total, bound, slope):
    if number_of == 2:
        one = jax.random.randint(rng, (), max(1, total - bound), min(bound, total - 1) + 1)
        return jnp.stack([one, total - one])
    tallies = jnp.asarray(length_profile(number_of, total, bound, slope), jnp.int32)
    couples = (number_of - 1) // 2
    donor, taker = tallies[1:1 + 2 * couples:2], tallies[2:2 + 2 * couples:2]
    room = jnp.minimum(donor - 1, bound - taker)
    moved = jax.random.randint(jax.random.fold_in(rng, 1), (couples,), 0, 1 << 20) % (room + 1)
    tallies = tallies.at[1:1 + 2 * couples:2].set(donor - moved).at[2:2 + 2 * couples:2].set(taker + moved)
    return tallies[jax.random.permutation(jax.random.fold_in(rng, 2), number_of)]


def centred(rng, shape, deviation, reach, split=(), kind=jnp.bfloat16):
    drawn = jax.random.normal(rng, shape, jnp.float32) * deviation
    if len(split) > 0:
        drawn = steps_of(rng, shape, split, -0.22, 0.18) * drawn
    return jnp.clip(drawn, min=-reach, max=reach).astype(kind)


def setup_inputs(seed: int = 0) -> dict:
    streams_of = jax.random.split(jax.random.key(seed), 9)
    queries = centred(streams_of[0], (TOKENS, HEADS * DH), 1.0, 6.0, ((0, 256),))
    grad_out = centred(streams_of[1], (TOKENS, HEADS * DH), 10.0, 60.0, ((0, 256),))
    attn_out = centred(streams_of[2], (TOKENS, HEADS * DH), 1.0, 6.0, ((0, 256),))
    saved_lse = jnp.clip(6.0 + 2.0 * jax.random.uniform(streams_of[3], (HEADS, TOKENS), jnp.float32) ** steps_of(streams_of[3], (HEADS, TOKENS), ((1, 256),), -0.2, 0.2), 6.0, 8.0)
    key_rows = centred(streams_of[4], (KEYS, DH), 1.0, 6.0, ((0, 256),))
    value_rows = centred(streams_of[5], (KEYS, DH), 1.0, 6.0, ((0, 256),))
    doc_lengths = ragged_sizes(streams_of[6], NDOC, KEYS, DOC_MOST, 2).astype(jnp.int32)
    read_steps = draw_read_steps(jax.random.fold_in(streams_of[8], 71), 0)
    return {"queries": queries, "grad_out": grad_out, "attn_out": attn_out, "saved_lse": saved_lse, "key_rows": key_rows, "value_rows": value_rows, "doc_lengths": doc_lengths, "read_steps": read_steps}


def doc_index(positions, doc_ends):
    return jnp.sum((doc_ends[None, :] <= positions[:, None]).astype(jnp.int32), axis=1)


def pair_grads(query_block, grad_block, lse_rows, delta_rows, key_block, value_block, allowed):
    row_count = query_block.shape[0]
    head_dim = key_block.shape[1]
    head_count = query_block.shape[1] // head_dim
    score_scale = head_dim ** -0.5
    query_flat = query_block.reshape(row_count * head_count, head_dim)
    grad_flat = grad_block.reshape(row_count * head_count, head_dim)
    visible = jnp.repeat(allowed, head_count, axis=0)
    scores = jnp.dot(query_flat, key_block.T, preferred_element_type=jnp.float32) * score_scale
    weights = jnp.where(visible, jnp.exp(scores - lse_rows[:, None]), 0.0)
    grad_weights = jnp.dot(grad_flat, value_block.T, preferred_element_type=jnp.float32)
    grad_scores = weights * (grad_weights - delta_rows[:, None])
    weight_half = weights.astype(jnp.bfloat16)
    score_half = grad_scores.astype(jnp.bfloat16)
    grad_query = jnp.dot(score_half, key_block, preferred_element_type=jnp.float32) * score_scale
    grad_key = jnp.dot(score_half.T, query_flat, preferred_element_type=jnp.float32) * score_scale
    grad_value = jnp.dot(weight_half.T, grad_flat, preferred_element_type=jnp.float32)
    return grad_query.reshape(row_count, head_count * head_dim), grad_key, grad_value


def reference(queries, grad_out, attn_out, saved_lse, key_rows, value_rows, doc_lengths, read_steps):
    device_count = KEYS // KB
    doc_ends = jnp.cumsum(doc_lengths, dtype=jnp.int32)
    row_delta = jnp.sum(grad_out.astype(jnp.float32).reshape(TOKENS, HEADS, DH) * attn_out.astype(jnp.float32).reshape(TOKENS, HEADS, DH), axis=2)
    query_iota = jnp.arange(Q_DEV, dtype=jnp.int32)
    key_iota = jnp.arange(KB, dtype=jnp.int32)
    grad_queries = jnp.zeros((TOKENS, HEADS * DH), jnp.float32)
    grad_keys = jnp.zeros((KEYS, DH), jnp.float32)
    grad_values = jnp.zeros((KEYS, DH), jnp.float32)
    for distance in range(STEPS):
        def one_device(device):
            owner_id = device - distance
            active = (owner_id >= 0) & (read_steps[device, distance] == owner_id)
            source = jnp.maximum(owner_id, 0).astype(jnp.int32)
            query_pos = device * KB + (KB - Q_DEV) + query_iota
            key_pos = source * KB + key_iota
            allowed = (doc_index(query_pos, doc_ends)[:, None] == doc_index(key_pos, doc_ends)[None, :]) & (key_pos[None, :] <= query_pos[:, None])
            query_block = lax.dynamic_slice_in_dim(queries, device * Q_DEV, Q_DEV, 0)
            grad_block = lax.dynamic_slice_in_dim(grad_out, device * Q_DEV, Q_DEV, 0)
            lse_rows = lax.dynamic_slice_in_dim(saved_lse, device * Q_DEV, Q_DEV, 1).T.reshape(-1)
            delta_rows = lax.dynamic_slice_in_dim(row_delta, device * Q_DEV, Q_DEV, 0).reshape(-1)
            key_block = lax.dynamic_slice_in_dim(key_rows, source * KB, KB, 0)
            value_block = lax.dynamic_slice_in_dim(value_rows, source * KB, KB, 0)

            def compute():
                return pair_grads(query_block, grad_block, lse_rows, delta_rows, key_block, value_block, allowed)

            def nothing():
                return (jnp.zeros((Q_DEV, HEADS * DH), jnp.float32), jnp.zeros((KB, DH), jnp.float32), jnp.zeros((KB, DH), jnp.float32))

            return lax.cond(active, compute, nothing)

        part_query, part_key, part_value = lax.map(one_device, jnp.arange(device_count, dtype=jnp.int32))
        grad_queries = grad_queries + part_query.reshape(TOKENS, HEADS * DH)
        padding = jnp.zeros((distance, KB, DH), jnp.float32)
        grad_keys = grad_keys + jnp.concatenate([part_key[distance:], padding], axis=0).reshape(KEYS, DH)
        grad_values = grad_values + jnp.concatenate([part_value[distance:], padding], axis=0).reshape(KEYS, DH)
    return grad_queries, grad_keys, grad_values
```

```python
import functools

import jax
import jax.numpy as jnp
from jax import lax
from jax.experimental import pallas as pl
from jax.experimental.pallas import tpu as pltpu
from jax.sharding import PartitionSpec as P

AXES = ("cpx", "cpy")
HEAD_DIM = 128
SCALE = HEAD_DIM**-0.5
LOG2E = 1.4426950408889634
KEY_TILE = 128
ROW_TILE = 512
LAST_BY_LAST = (((1,), (1,)), ((), ()))
FIRST_BY_FIRST = (((0,), (0,)), ((), ()))
F32, BF16, I32 = jnp.float32, jnp.bfloat16, jnp.int32


def passed_along(value, steps):
    count = lax.axis_size(AXES)
    return lax.ppermute(value, AXES, [(d, (d + steps) % count) for d in range(count)])


def make_weights(distance, k_ref, v_ref, q_ref, g_ref, stats_ref, w_ref, s_ref):
    block, flat = w_ref.shape
    rows = flat // 8

    def columns(j, carry):
        cs = pl.ds(pl.multiple_of(j * ROW_TILE, ROW_TILE), ROW_TILE)
        q, g = q_ref[cs, :], g_ref[cs, :]
        lse, delta = stats_ref[0:1, cs], stats_ref[1:2, cs]
        first_key = stats_ref[2:3, cs] + float(distance * block)
        for i in range(block // KEY_TILE):
            ks = slice(i * KEY_TILE, (i + 1) * KEY_TILE)
            scores = lax.dot_general(k_ref[ks, :], q, LAST_BY_LAST, preferred_element_type=F32)
            grad_w = lax.dot_general(v_ref[ks, :], g, LAST_BY_LAST, preferred_element_type=F32)
            key = (lax.broadcasted_iota(I32, (KEY_TILE, ROW_TILE), 0) + i * KEY_TILE).astype(F32)
            allowed = key >= first_key
            if distance == 0 and (i + 1) * KEY_TILE > block - rows:
                allowed = allowed & (key <= stats_ref[3:4, cs])
            weights = jnp.where(allowed, jnp.exp2(scores * (SCALE * LOG2E) - lse), 0.0)
            w_ref[ks, cs] = weights.astype(BF16)
            s_ref[ks, cs] = (weights * (grad_w - delta)).astype(BF16)
        return carry

    lax.fori_loop(0, flat // ROW_TILE, columns, 0)


def key_value_grads(q_ref, g_ref, w_ref, s_ref, dk_ref, dv_ref):
    dk = jnp.dot(s_ref[...], q_ref[...], preferred_element_type=F32) * SCALE
    dk_ref[...] = dk.astype(dk_ref.dtype)
    dv_ref[...] = jnp.dot(w_ref[...], g_ref[...], preferred_element_type=F32).astype(dv_ref.dtype)


def query_grads(k_ref, s_ref):
    return lax.dot_general(k_ref[...], s_ref[...], FIRST_BY_FIRST, preferred_element_type=F32) * SCALE


def own_kernel(
    lens_hbm, steps_hbm, q_hbm, g_hbm, o_hbm, lse_hbm, k_hbm, v_hbm,
    q_ref, g_ref, stats_ref, flags_ref, dk_ref, dv_ref, dq_ref,
    o_ref, w_ref, s_ref, lse_ref, k_ref, v_ref, lens_ref, steps_ref, head_sems, sems,
):
    rows = q_hbm.shape[0]
    block, head_dim = k_hbm.shape
    heads = q_hbm.shape[1] // head_dim
    flat = rows * heads
    device = lax.axis_index(AXES)
    whole = [
        pltpu.make_async_copy(source, target, sems.at[i])
        for i, (source, target) in enumerate(
            [
                (lens_hbm, lens_ref),
                (steps_hbm, steps_ref),
                (lse_hbm, lse_ref),
                (k_hbm, k_ref),
                (v_hbm, v_ref),
            ]
        )
    ]
    by_head = [
        pltpu.make_async_copy(
            source.at[:, h * head_dim : (h + 1) * head_dim],
            target.at[h * rows : (h + 1) * rows, :],
            head_sems.at[i, h],
        )
        for i, (source, target) in enumerate([(g_hbm, g_ref), (o_hbm, o_ref), (q_hbm, q_ref)])
        for h in range(heads)
    ]
    for copy in whole + by_head:
        copy.start()
    for copy in whole + by_head:
        copy.wait()
    for h in range(heads):
        stats_ref[0:1, h * rows : (h + 1) * rows] = lse_ref[h : h + 1, :] * LOG2E
    for c in range(flat // 128):
        cs = slice(c * 128, (c + 1) * 128)
        product = g_ref[cs, :].astype(F32) * o_ref[cs, :].astype(F32)
        stats_ref[1:2, cs] = jnp.sum(product.T, axis=0, keepdims=True)
    column = lax.broadcasted_iota(I32, (1, flat), 1)
    head = jnp.zeros((1, flat), I32)
    for h in range(1, heads):
        head = head + (column >= h * rows).astype(I32)
    local = column - head * rows + (block - rows)
    base = device * block
    query_pos = local + base

    def one_end(i, carry):
        end, starts, first = carry
        end = end + lens_ref[i]
        starts = jnp.where(query_pos >= end, end, starts)
        first = jnp.where(base + (block - rows) >= end, end, first)
        return end, starts, first

    zero = jnp.int32(0)
    _, starts, first = lax.fori_loop(
        0, lens_ref.shape[0], one_end, (zero, jnp.zeros((1, flat), I32), zero)
    )
    stats_ref[2:3, :] = (starts - base).astype(F32)
    stats_ref[3:4, :] = local.astype(F32)
    for t in range(steps_ref.shape[0]):
        owner = device - t
        active = (owner >= 0) & (steps_ref[t, device] == owner) & (first < (owner + 1) * block)
        flags_ref[t] = active.astype(I32)

    @pl.when(flags_ref[0] == 1)
    def _():
        make_weights(0, k_ref, v_ref, q_ref, g_ref, stats_ref, w_ref, s_ref)
        key_value_grads(q_ref, g_ref, w_ref, s_ref, dk_ref, dv_ref)
        dq_ref[...] = query_grads(k_ref, s_ref)

    @pl.when(flags_ref[0] == 0)
    def _():
        dk_ref[...] = jnp.zeros_like(dk_ref)
        dv_ref[...] = jnp.zeros_like(dv_ref)
        dq_ref[...] = jnp.zeros_like(dq_ref)


def block_kernel(
    distance, flags_ref, stats_ref, q_ref, g_ref, k_ref, v_ref, dq_in,
    dk_ref, dv_ref, dq_ref, w_ref, s_ref,
):
    @pl.when(flags_ref[distance] == 1)
    def _():
        make_weights(distance, k_ref, v_ref, q_ref, g_ref, stats_ref, w_ref, s_ref)
        key_value_grads(q_ref, g_ref, w_ref, s_ref, dk_ref, dv_ref)
        dq_ref[...] = dq_in[...] + query_grads(k_ref, s_ref)

    @pl.when(flags_ref[distance] == 0)
    def _():
        dk_ref[...] = jnp.zeros_like(dk_ref)
        dv_ref[...] = jnp.zeros_like(dv_ref)
        dq_ref[...] = dq_in[...]


def last_block_kernel(
    distance, flags_ref, stats_ref, q_ref, g_ref, k_ref, v_ref, dk_ref, dv_ref, s_ref, w_ref
):
    @pl.when(flags_ref[distance] == 1)
    def _():
        make_weights(distance, k_ref, v_ref, q_ref, g_ref, stats_ref, w_ref, s_ref)
        key_value_grads(q_ref, g_ref, w_ref, s_ref, dk_ref, dv_ref)

    @pl.when(flags_ref[distance] == 0)
    def _():
        dk_ref[...] = jnp.zeros_like(dk_ref)
        dv_ref[...] = jnp.zeros_like(dv_ref)


def queries_kernel(distance, flags_ref, k_ref, s_ref, dq_in, out_ref, dq_ref):
    rows, width = out_ref.shape
    head_dim = k_ref.shape[1]
    dq_ref[...] = dq_in[...]

    @pl.when(flags_ref[distance] == 1)
    def _():
        dq_ref[...] += query_grads(k_ref, s_ref)

    by_row = dq_ref[...].T
    for h in range(width // head_dim):
        out_ref[:, h * head_dim : (h + 1) * head_dim] = by_row[h * rows : (h + 1) * rows, :]


def call(kernel, name, outs, scratch, args, places=None, smem_outs=(), aliases=None, limit=40):
    vmem, smem = pl.BlockSpec(memory_space=pltpu.VMEM), pl.BlockSpec(memory_space=pltpu.SMEM)
    if places is None:
        places = [smem] + [vmem] * (len(args) - 1)
    return pl.pallas_call(
        kernel,
        name=name,
        out_shape=[jax.ShapeDtypeStruct(s, d) for s, d in outs],
        in_specs=places,
        out_specs=[smem if i in smem_outs else vmem for i in range(len(outs))],
        scratch_shapes=scratch,
        input_output_aliases=aliases or {},
        cost_estimate=pl.CostEstimate(flops=0, bytes_accessed=0, transcendentals=0),
        compiler_params=pltpu.CompilerParams(vmem_limit_bytes=limit << 20),
    )(*args)


def local(queries, grad_out, attn_out, saved_lse, key_rows, value_rows, doc_lengths, read_steps):
    rows, width = queries.shape
    block, head_dim = key_rows.shape
    heads = width // head_dim
    flat = rows * heads
    half = ((block, head_dim), BF16)
    full = ((block, head_dim), F32)
    scores = ((block, flat), BF16)
    flat_rows = ((flat, head_dim), BF16)
    total = ((head_dim, flat), F32)
    scores_scratch = pltpu.VMEM(*scores)
    own = (doc_lengths, read_steps.T, queries, grad_out, attn_out, saved_lse, key_rows, value_rows)

    k1 = passed_along(key_rows, 1)
    v3 = passed_along(value_rows, 3)
    v1 = passed_along(value_rows, 1)
    k3 = passed_along(key_rows, 3)
    q, g, stats, flags, dk0, dv0, dq = call(
        own_kernel, "own_block",
        [flat_rows, flat_rows, ((8, flat), F32), ((8,), I32), full, full, total],
        [
            pltpu.VMEM(*flat_rows), scores_scratch, scores_scratch, pltpu.VMEM((heads, rows), F32),
            pltpu.VMEM(*half), pltpu.VMEM(*half),
            pltpu.SMEM(own[0].shape, I32), pltpu.SMEM(own[1].shape, I32),
            pltpu.SemaphoreType.DMA((3, heads)), pltpu.SemaphoreType.DMA((5,)),
        ],
        own, [pl.BlockSpec(memory_space=pltpu.HBM)] * 8, smem_outs=(3,), limit=54,
    )
    k1, v3, flags = lax.optimization_barrier((k1, v3, flags))
    k2 = passed_along(k1, 1)
    v2 = passed_along(v3, -1)

    def other(distance, k, v, dq, outs):
        return call(
            functools.partial(block_kernel, distance), f"block_{distance}",
            [*outs, total], [scores_scratch] * 2, (flags, stats, q, g, k, v, dq),
        )

    dk1, dv1, dq = other(1, k1, v1, dq, [full, half])
    dv1 = passed_along(dv1, -1)
    dk3, dv3, dq = other(3, k3, v3, dq, [half, full])
    dk3 = passed_along(dk3, -3)
    k2, v2, dq = lax.optimization_barrier((k2, v2, dq))
    dk2, dv2, s2 = call(
        functools.partial(last_block_kernel, 2), "block_2",
        [half, half, scores], [scores_scratch], (flags, stats, q, g, k2, v2),
    )
    dk2 = passed_along(dk2, -1)
    dv2 = passed_along(dv2, 1)
    dv1, dk3, dq = lax.optimization_barrier((dv1, dk3, dq))
    (grad_queries,) = call(
        functools.partial(queries_kernel, 2), "queries",
        [((rows, width), F32)], [pltpu.VMEM(*total)], (flags, k2, s2, dq),
    )
    dk1 = passed_along((dk1 + dk2.astype(F32)).astype(BF16), -1)
    dv3 = passed_along((dv3 + dv2.astype(F32)).astype(BF16), -3)
    grad_keys = dk0 + dk3.astype(F32) + dk1.astype(F32)
    grad_values = dv0 + dv1.astype(F32) + dv3.astype(F32)
    return grad_queries, grad_keys, grad_values


def solution(mesh):
    return jax.shard_map(
        local,
        mesh=mesh,
        in_specs=(
            P(AXES, None),
            P(AXES, None),
            P(AXES, None),
            P(None, AXES),
            P(AXES, None),
            P(AXES, None),
            P(),
            P(),
        ),
        out_specs=(P(AXES, None), P(AXES, None), P(AXES, None)),
        check_vma=False,
    )
```

```python
import functools

import jax
import jax.numpy as jnp
from jax import lax
from jax.experimental import pallas as pl
from jax.experimental.pallas import tpu as pltpu
from jax.sharding import PartitionSpec as P

AXES = ("cpx", "cpy")
HEAD_DIM = 128
SCALE = HEAD_DIM**-0.5
LOG2E = 1.4426950408889634
KEY_TILE = 128
ROW_TILE = 512
LAST_BY_LAST = (((1,), (1,)), ((), ()))
FIRST_BY_FIRST = (((0,), (0,)), ((), ()))
F32, BF16, I32 = jnp.float32, jnp.bfloat16, jnp.int32


def passed_along(value, steps):
    count = lax.axis_size(AXES)
    return lax.ppermute(value, AXES, [(d, (d + steps) % count) for d in range(count)])


def make_weights(distance, k_ref, v_ref, q_ref, g_ref, stats_ref, w_ref, s_ref):
    block, flat = w_ref.shape
    rows = flat // 8

    def columns(j, carry):
        cs = pl.ds(pl.multiple_of(j * ROW_TILE, ROW_TILE), ROW_TILE)
        q, g = q_ref[cs, :], g_ref[cs, :]
        lse, delta = stats_ref[0:1, cs], stats_ref[1:2, cs]
        first_key = stats_ref[2:3, cs] + float(distance * block)
        for i in range(block // KEY_TILE):
            ks = slice(i * KEY_TILE, (i + 1) * KEY_TILE)
            scores = lax.dot_general(k_ref[ks, :], q, LAST_BY_LAST, preferred_element_type=F32)
            grad_w = lax.dot_general(v_ref[ks, :], g, LAST_BY_LAST, preferred_element_type=F32)
            key = (lax.broadcasted_iota(I32, (KEY_TILE, ROW_TILE), 0) + i * KEY_TILE).astype(F32)
            allowed = key >= first_key
            if distance == 0 and (i + 1) * KEY_TILE > block - rows:
                allowed = allowed & (key <= stats_ref[3:4, cs])
            weights = jnp.where(allowed, jnp.exp2(scores * (SCALE * LOG2E) - lse), 0.0)
            w_ref[ks, cs] = weights.astype(BF16)
            s_ref[ks, cs] = (weights * (grad_w - delta)).astype(BF16)
        return carry

    lax.fori_loop(0, flat // ROW_TILE, columns, 0)


def key_value_grads(q_ref, g_ref, w_ref, s_ref, dk_ref, dv_ref):
    dk = jnp.dot(s_ref[...], q_ref[...], preferred_element_type=F32) * SCALE
    dk_ref[...] = dk.astype(dk_ref.dtype)
    dv_ref[...] = jnp.dot(w_ref[...], g_ref[...], preferred_element_type=F32).astype(dv_ref.dtype)


def query_grads(k_ref, s_ref):
    return lax.dot_general(k_ref[...], s_ref[...], FIRST_BY_FIRST, preferred_element_type=F32) * SCALE


def prepare_kernel(
    lens_hbm, steps_hbm, q_hbm, g_hbm, o_hbm, lse_hbm,
    q_ref, g_ref, stats_ref, flags_ref,
    o_ref, lse_ref, lens_ref, steps_ref, head_sems, sems, *, block,
):
    rows = q_hbm.shape[0]
    flat, head_dim = q_ref.shape
    heads = flat // rows
    device = lax.axis_index(AXES)
    small = [
        pltpu.make_async_copy(source, target, sems.at[i])
        for i, (source, target) in enumerate(
            [(lens_hbm, lens_ref), (steps_hbm, steps_ref), (lse_hbm, lse_ref)]
        )
    ]
    g_copies, o_copies, q_copies = (
        [
            pltpu.make_async_copy(
                source.at[:, h * head_dim : (h + 1) * head_dim],
                target.at[h * rows : (h + 1) * rows, :],
                head_sems.at[i, h],
            )
            for h in range(heads)
        ]
        for i, (source, target) in enumerate([(g_hbm, g_ref), (o_hbm, o_ref), (q_hbm, q_ref)])
    )
    for copy in small + g_copies + o_copies + q_copies:
        copy.start()
    for copy in small:
        copy.wait()
    for h in range(heads):
        stats_ref[0:1, h * rows : (h + 1) * rows] = lse_ref[h : h + 1, :] * LOG2E
    column = lax.broadcasted_iota(I32, (1, flat), 1)
    head = jnp.zeros((1, flat), I32)
    for h in range(1, heads):
        head = head + (column >= h * rows).astype(I32)
    local = column - head * rows + (block - rows)
    base = device * block
    query_pos = local + base

    def one_end(i, carry):
        end, starts, first = carry
        end = end + lens_ref[i]
        starts = jnp.where(query_pos >= end, end, starts)
        first = jnp.where(base + (block - rows) >= end, end, first)
        return end, starts, first

    zero = jnp.int32(0)
    _, starts, first = lax.fori_loop(
        0, lens_ref.shape[0], one_end, (zero, jnp.zeros((1, flat), I32), zero)
    )
    stats_ref[2:3, :] = (starts - base).astype(F32)
    stats_ref[3:4, :] = local.astype(F32)
    for t in range(steps_ref.shape[0]):
        owner = device - t
        active = (owner >= 0) & (steps_ref[t, device] == owner) & (first < (owner + 1) * block)
        flags_ref[t] = active.astype(I32)
    for copy in g_copies + o_copies:
        copy.wait()
    for c in range(flat // 128):
        cs = slice(c * 128, (c + 1) * 128)
        product = g_ref[cs, :].astype(F32) * o_ref[cs, :].astype(F32)
        stats_ref[1:2, cs] = jnp.sum(product.T, axis=0, keepdims=True)
    for copy in q_copies:
        copy.wait()


def block_kernel(
    distance, flags_ref, stats_ref, q_ref, g_ref, k_ref, v_ref, dk_ref, dv_ref, s_ref, w_ref
):
    @pl.when(flags_ref[distance] == 1)
    def _():
        make_weights(distance, k_ref, v_ref, q_ref, g_ref, stats_ref, w_ref, s_ref)
        key_value_grads(q_ref, g_ref, w_ref, s_ref, dk_ref, dv_ref)

    @pl.when(flags_ref[distance] == 0)
    def _():
        dk_ref[...] = jnp.zeros_like(dk_ref)
        dv_ref[...] = jnp.zeros_like(dv_ref)


def queries_kernel(flags_ref, *refs):
    count = (len(refs) - 2) // 2
    k_refs, s_refs, (out_ref, dq_ref) = refs[:count], refs[count : 2 * count], refs[2 * count :]
    rows, width = out_ref.shape
    head_dim = k_refs[0].shape[1]
    dq_ref[...] = jnp.zeros_like(dq_ref)
    for t in range(count):

        @pl.when(flags_ref[t] == 1)
        def _(t=t):
            dq_ref[...] += query_grads(k_refs[t], s_refs[t])

    by_row = dq_ref[...].T
    for h in range(width // head_dim):
        out_ref[:, h * head_dim : (h + 1) * head_dim] = by_row[h * rows : (h + 1) * rows, :]


def call(kernel, name, outs, scratch, args, places=None, smem_outs=(), flops=0, limit=40 << 20):
    vmem, smem = pl.BlockSpec(memory_space=pltpu.VMEM), pl.BlockSpec(memory_space=pltpu.SMEM)
    if places is None:
        places = [smem] + [vmem] * (len(args) - 1)
    return pl.pallas_call(
        kernel,
        name=name,
        out_shape=[jax.ShapeDtypeStruct(s, d) for s, d in outs],
        in_specs=places,
        out_specs=[smem if i in smem_outs else vmem for i in range(len(outs))],
        scratch_shapes=scratch,
        cost_estimate=pl.CostEstimate(flops=flops, bytes_accessed=0, transcendentals=0),
        compiler_params=pltpu.CompilerParams(vmem_limit_bytes=limit),
    )(*args)


def local(queries, grad_out, attn_out, saved_lse, key_rows, value_rows, doc_lengths, read_steps):
    rows, width = queries.shape
    block, head_dim = key_rows.shape
    heads = width // head_dim
    flat = rows * heads
    half = ((block, head_dim), BF16)
    full = ((block, head_dim), F32)
    scores = ((block, flat), BF16)
    flat_rows = ((flat, head_dim), BF16)
    total = ((head_dim, flat), F32)
    given = (doc_lengths, read_steps.T, queries, grad_out, attn_out, saved_lse)

    k1 = passed_along(key_rows, 1)
    v3 = passed_along(value_rows, 3)
    q, g, stats, flags = call(
        functools.partial(prepare_kernel, block=block), "prepare",
        [flat_rows, flat_rows, ((8, flat), F32), ((8,), I32)],
        [
            pltpu.VMEM(*flat_rows), pltpu.VMEM((heads, rows), F32),
            pltpu.SMEM(given[0].shape, I32), pltpu.SMEM(given[1].shape, I32),
            pltpu.SemaphoreType.DMA((3, heads)), pltpu.SemaphoreType.DMA((3,)),
        ],
        given, [pl.BlockSpec(memory_space=pltpu.HBM)] * 6, smem_outs=(3,), flops=20_000_000_000, limit=211 << 18,
    )

    def grads(distance, k, v, outs):
        return call(
            functools.partial(block_kernel, distance), f"block_{distance}",
            [*outs, scores], [pltpu.VMEM(*scores)], (flags, stats, q, g, k, v),
        )

    k1, v3, flags = lax.optimization_barrier((k1, v3, flags))
    k2 = passed_along(k1, 1)
    v2 = passed_along(v3, -1)
    key_rows, value_rows, flags = lax.optimization_barrier((key_rows, value_rows, flags))
    v1 = passed_along(value_rows, 1)
    k3 = passed_along(key_rows, 3)
    dk0, dv0, s0 = grads(0, key_rows, value_rows, [full, full])
    k2, v2, s0 = lax.optimization_barrier((k2, v2, s0))
    dk2, dv2, s2 = grads(2, k2, v2, [half, half])
    dk2r = passed_along(dk2, -1)
    dv2r = passed_along(dv2, 1)
    v1, s2 = lax.optimization_barrier((v1, s2))
    dk1, dv1, s1 = grads(1, k1, v1, [full, half])
    dv1r = passed_along(dv1, -1)
    k3, s1 = lax.optimization_barrier((k3, s1))
    dk3, dv3, s3 = grads(3, k3, v3, [half, full])
    dk3r = passed_along(dk3, -3)
    dk2r, dv2r, flags = lax.optimization_barrier((dk2r, dv2r, flags))
    dk1r = passed_along((dk1 + dk2r.astype(F32)).astype(BF16), -1)
    dv3r = passed_along((dv3 + dv2r.astype(F32)).astype(BF16), -3)
    (grad_queries,) = call(
        queries_kernel, "queries",
        [((rows, width), F32)], [pltpu.VMEM(*total)],
        (flags, key_rows, k1, k2, k3, s0, s1, s2, s3),
    )
    grad_keys = dk0 + dk3r.astype(F32) + dk1r.astype(F32)
    grad_values = dv0 + dv1r.astype(F32) + dv3r.astype(F32)
    return grad_queries, grad_keys, grad_values


def solution(mesh):
    return jax.shard_map(
        local,
        mesh=mesh,
        in_specs=(
            P(AXES, None),
            P(AXES, None),
            P(AXES, None),
            P(None, AXES),
            P(AXES, None),
            P(AXES, None),
            P(),
            P(),
        ),
        out_specs=(P(AXES, None), P(AXES, None), P(AXES, None)),
        check_vma=False,
    )
```

```python
import functools

import jax
import jax.numpy as jnp
from jax import lax
from jax.experimental import pallas as pl
from jax.experimental.pallas import tpu as pltpu
from jax.sharding import PartitionSpec as P

AXES = ("cpx", "cpy")
HEAD_DIM = 128
SCALE = HEAD_DIM**-0.5
LOG2E = 1.4426950408889634
KEY_TILE = 128
ROW_TILE = 512
LAST_BY_LAST = (((1,), (1,)), ((), ()))
FIRST_BY_FIRST = (((0,), (0,)), ((), ()))
F32, BF16, I32 = jnp.float32, jnp.bfloat16, jnp.int32


def passed_along(value, steps):
    count = lax.axis_size(AXES)
    return lax.ppermute(value, AXES, [(d, (d + steps) % count) for d in range(count)])


def make_weights(distance, k_ref, v_ref, q_ref, g_ref, stats_ref, w_ref, s_ref):
    block, flat = w_ref.shape
    rows = flat // 8

    for j in range(flat // ROW_TILE):
        cs = slice(j * ROW_TILE, (j + 1) * ROW_TILE)
        q, g = q_ref[cs, :], g_ref[cs, :]
        lse, delta = stats_ref[0:1, cs], stats_ref[1:2, cs]
        first_key = stats_ref[2:3, cs] + float(distance * block)
        for i in range(block // KEY_TILE):
            ks = slice(i * KEY_TILE, (i + 1) * KEY_TILE)
            scores = lax.dot_general(k_ref[ks, :], q, LAST_BY_LAST, preferred_element_type=F32)
            grad_w = lax.dot_general(v_ref[ks, :], g, LAST_BY_LAST, preferred_element_type=F32)
            key = (lax.broadcasted_iota(I32, (KEY_TILE, ROW_TILE), 0) + i * KEY_TILE).astype(F32)
            allowed = key >= first_key
            if distance == 0 and (i + 1) * KEY_TILE > block - rows:
                allowed = allowed & (key <= stats_ref[3:4, cs])
            weights = jnp.where(allowed, jnp.exp2(scores * (SCALE * LOG2E) - lse), 0.0)
            w_ref[ks, cs] = weights.astype(BF16)
            s_ref[ks, cs] = (weights * (grad_w - delta)).astype(BF16)


def key_value_grads(q_ref, g_ref, w_ref, s_ref, dk_ref, dv_ref):
    dk = jnp.dot(s_ref[...], q_ref[...], preferred_element_type=F32) * SCALE
    dk_ref[...] = dk.astype(dk_ref.dtype)
    dv_ref[...] = jnp.dot(w_ref[...], g_ref[...], preferred_element_type=F32).astype(dv_ref.dtype)


def query_grads(k_ref, s_ref):
    return lax.dot_general(k_ref[...], s_ref[...], FIRST_BY_FIRST, preferred_element_type=F32) * SCALE


def prepare_kernel(
    lens_hbm, steps_hbm, q_hbm, g_hbm, o_hbm, lse_hbm,
    q_ref, g_ref, stats_ref, flags_ref,
    o_ref, lse_ref, lens_ref, steps_ref, head_sems, sems, *, block,
):
    rows = q_hbm.shape[0]
    flat, head_dim = q_ref.shape
    heads = flat // rows
    device = lax.axis_index(AXES)
    small = [
        pltpu.make_async_copy(source, target, sems.at[i])
        for i, (source, target) in enumerate(
            [(lens_hbm, lens_ref), (steps_hbm, steps_ref), (lse_hbm, lse_ref)]
        )
    ]
    g_copies, o_copies, q_copies = (
        [
            pltpu.make_async_copy(
                source.at[:, h * head_dim : (h + 1) * head_dim],
                target.at[h * rows : (h + 1) * rows, :],
                head_sems.at[i, h],
            )
            for h in range(heads)
        ]
        for i, (source, target) in enumerate([(g_hbm, g_ref), (o_hbm, o_ref), (q_hbm, q_ref)])
    )
    for copy in small + g_copies + o_copies + q_copies:
        copy.start()
    for copy in small:
        copy.wait()
    for h in range(heads):
        stats_ref[0:1, h * rows : (h + 1) * rows] = lse_ref[h : h + 1, :] * LOG2E
    column = lax.broadcasted_iota(I32, (1, flat), 1)
    head = jnp.zeros((1, flat), I32)
    for h in range(1, heads):
        head = head + (column >= h * rows).astype(I32)
    local = column - head * rows + (block - rows)
    base = device * block
    query_pos = local + base

    def one_end(i, carry):
        end, starts, first = carry
        end = end + lens_ref[i]
        starts = jnp.where(query_pos >= end, end, starts)
        first = jnp.where(base + (block - rows) >= end, end, first)
        return end, starts, first

    zero = jnp.int32(0)
    _, starts, first = lax.fori_loop(
        0, lens_ref.shape[0], one_end, (zero, jnp.zeros((1, flat), I32), zero)
    )
    stats_ref[2:3, :] = (starts - base).astype(F32)
    stats_ref[3:4, :] = local.astype(F32)
    for t in range(steps_ref.shape[0]):
        owner = device - t
        active = (owner >= 0) & (steps_ref[t, device] == owner) & (first < (owner + 1) * block)
        flags_ref[t] = active.astype(I32)
    for copy in g_copies + o_copies:
        copy.wait()
    for c in range(flat // 128):
        cs = slice(c * 128, (c + 1) * 128)
        product = g_ref[cs, :].astype(F32) * o_ref[cs, :].astype(F32)
        stats_ref[1:2, cs] = jnp.sum(product.T, axis=0, keepdims=True)
    for copy in q_copies:
        copy.wait()


def block_kernel(
    distance, flags_ref, stats_ref, q_ref, g_ref, k_ref, v_ref, dk_ref, dv_ref, s_ref, w_ref
):
    @pl.when(flags_ref[distance] == 1)
    def _():
        make_weights(distance, k_ref, v_ref, q_ref, g_ref, stats_ref, w_ref, s_ref)
        key_value_grads(q_ref, g_ref, w_ref, s_ref, dk_ref, dv_ref)

    @pl.when(flags_ref[distance] == 0)
    def _():
        dk_ref[...] = jnp.zeros_like(dk_ref)
        dv_ref[...] = jnp.zeros_like(dv_ref)


def queries_kernel(flags_ref, *refs):
    count = (len(refs) - 2) // 2
    k_refs, s_refs, (out_ref, dq_ref) = refs[:count], refs[count : 2 * count], refs[2 * count :]
    rows, width = out_ref.shape
    head_dim = k_refs[0].shape[1]
    dq_ref[...] = jnp.zeros_like(dq_ref)
    for t in range(count):

        @pl.when(flags_ref[t] == 1)
        def _(t=t):
            dq_ref[...] += query_grads(k_refs[t], s_refs[t])

    by_row = dq_ref[...].T
    for h in range(width // head_dim):
        out_ref[:, h * head_dim : (h + 1) * head_dim] = by_row[h * rows : (h + 1) * rows, :]


def call(kernel, name, outs, scratch, args, places=None, smem_outs=(), flops=0, limit=40 << 20):
    vmem, smem = pl.BlockSpec(memory_space=pltpu.VMEM), pl.BlockSpec(memory_space=pltpu.SMEM)
    if places is None:
        places = [smem] + [vmem] * (len(args) - 1)
    return pl.pallas_call(
        kernel,
        name=name,
        out_shape=[jax.ShapeDtypeStruct(s, d) for s, d in outs],
        in_specs=places,
        out_specs=[smem if i in smem_outs else vmem for i in range(len(outs))],
        scratch_shapes=scratch,
        cost_estimate=pl.CostEstimate(flops=flops, bytes_accessed=0, transcendentals=0),
        compiler_params=pltpu.CompilerParams(vmem_limit_bytes=limit),
    )(*args)


def local(queries, grad_out, attn_out, saved_lse, key_rows, value_rows, doc_lengths, read_steps):
    rows, width = queries.shape
    block, head_dim = key_rows.shape
    heads = width // head_dim
    flat = rows * heads
    half = ((block, head_dim), BF16)
    full = ((block, head_dim), F32)
    scores = ((block, flat), BF16)
    flat_rows = ((flat, head_dim), BF16)
    total = ((head_dim, flat), F32)
    given = (doc_lengths, read_steps.T, queries, grad_out, attn_out, saved_lse)

    k1 = passed_along(key_rows, 1)
    v3 = passed_along(value_rows, 3)
    q, g, stats, flags = call(
        functools.partial(prepare_kernel, block=block), "prepare",
        [flat_rows, flat_rows, ((8, flat), F32), ((8,), I32)],
        [
            pltpu.VMEM(*flat_rows), pltpu.VMEM((heads, rows), F32),
            pltpu.SMEM(given[0].shape, I32), pltpu.SMEM(given[1].shape, I32),
            pltpu.SemaphoreType.DMA((3, heads)), pltpu.SemaphoreType.DMA((3,)),
        ],
        given, [pl.BlockSpec(memory_space=pltpu.HBM)] * 6, smem_outs=(3,), flops=20_000_000_000, limit=211 << 18,
    )

    def grads(distance, k, v, outs):
        return call(
            functools.partial(block_kernel, distance), f"block_{distance}",
            [*outs, scores], [pltpu.VMEM(*scores)], (flags, stats, q, g, k, v),
        )

    key_late, value_late, flags = lax.optimization_barrier((key_rows, value_rows, flags))
    v1 = passed_along(value_late, 1)
    k3 = passed_along(key_late, 3)
    dk0, dv0, s0 = grads(0, key_rows, value_rows, [full, full])
    k1, v3, s0 = lax.optimization_barrier((k1, v3, s0))
    k2 = passed_along(k1, 1)
    v2 = passed_along(v3, -1)
    v1, s0 = lax.optimization_barrier((v1, s0))
    dk1, dv1, s1 = grads(1, k1, v1, [full, half])
    dv1r = passed_along(dv1, -1)
    k2, v2, k3, s1 = lax.optimization_barrier((k2, v2, k3, s1))
    dk2, dv2, s2 = grads(2, k2, v2, [half, half])
    dk2r = passed_along(dk2, -1)
    dv2r = passed_along(dv2, 1)
    k3, s2, dv1r = lax.optimization_barrier((k3, s2, dv1r))
    dk3, dv3, s3 = grads(3, k3, v3, [half, full])
    dk3r = passed_along(dk3, -3)
    dv2r, dk2r, flags = lax.optimization_barrier((dv2r, dk2r, flags))
    dv3 = (dv3 + dv2r.astype(F32)).astype(BF16)
    dk2r, dv3 = lax.optimization_barrier((dk2r, dv3))
    dv3r = passed_along(dv3, -3)
    dk1r = passed_along((dk1 + dk2r.astype(F32)).astype(BF16), -1)
    (grad_queries,) = call(
        queries_kernel, "queries",
        [((rows, width), F32)], [pltpu.VMEM(*total)],
        (flags, key_rows, k1, k2, k3, s0, s1, s2, s3),
    )
    grad_keys = dk0 + dk3r.astype(F32) + dk1r.astype(F32)
    grad_values = dv0 + dv1r.astype(F32) + dv3r.astype(F32)
    return grad_queries, grad_keys, grad_values


def solution(mesh):
    return jax.shard_map(
        local,
        mesh=mesh,
        in_specs=(
            P(AXES, None),
            P(AXES, None),
            P(AXES, None),
            P(None, AXES),
            P(AXES, None),
            P(AXES, None),
            P(),
            P(),
        ),
        out_specs=(P(AXES, None), P(AXES, None), P(AXES, None)),
        check_vma=False,
    )
```

```python
import functools

import jax
import jax.numpy as jnp
from jax import lax
from jax.experimental import pallas as pl
from jax.experimental.pallas import tpu as pltpu
from jax.sharding import PartitionSpec as P

AXES = ("cpx", "cpy")
HEAD_DIM = 128
SCALE = HEAD_DIM**-0.5
LOG2E = 1.4426950408889634
KEY_TILE = 128
ROW_TILE = 512
LAST_BY_LAST = (((1,), (1,)), ((), ()))
FIRST_BY_FIRST = (((0,), (0,)), ((), ()))
F32, BF16, I32 = jnp.float32, jnp.bfloat16, jnp.int32


def passed_along(value, steps):
    count = lax.axis_size(AXES)
    return lax.ppermute(value, AXES, [(d, (d + steps) % count) for d in range(count)])


def make_weights(distance, k_ref, v_ref, q_ref, g_ref, stats_ref, w_ref, s_ref):
    block, flat = w_ref.shape
    rows = flat // 8

    for j in range(flat // ROW_TILE):
        cs = slice(j * ROW_TILE, (j + 1) * ROW_TILE)
        q, g = q_ref[cs, :], g_ref[cs, :]
        lse, delta = stats_ref[0:1, cs], stats_ref[1:2, cs]
        first_key = stats_ref[2:3, cs] + float(distance * block)
        for i in range(block // KEY_TILE):
            ks = slice(i * KEY_TILE, (i + 1) * KEY_TILE)
            scores = lax.dot_general(k_ref[ks, :], q, LAST_BY_LAST, preferred_element_type=F32)
            grad_w = lax.dot_general(v_ref[ks, :], g, LAST_BY_LAST, preferred_element_type=F32)
            key = (lax.broadcasted_iota(I32, (KEY_TILE, ROW_TILE), 0) + i * KEY_TILE).astype(F32)
            allowed = key >= first_key
            if distance == 0 and (i + 1) * KEY_TILE > block - rows:
                allowed = allowed & (key <= stats_ref[3:4, cs])
            weights = jnp.where(allowed, jnp.exp2(scores * (SCALE * LOG2E) - lse), 0.0)
            w_ref[ks, cs] = weights.astype(BF16)
            s_ref[ks, cs] = (weights * (grad_w - delta)).astype(BF16)


def key_value_grads(q_ref, g_ref, w_ref, s_ref, dk_ref, dv_ref):
    dk = jnp.dot(s_ref[...], q_ref[...], preferred_element_type=F32) * SCALE
    dk_ref[...] = dk.astype(dk_ref.dtype)
    dv_ref[...] = jnp.dot(w_ref[...], g_ref[...], preferred_element_type=F32).astype(dv_ref.dtype)


def query_grads(k_ref, s_ref):
    return lax.dot_general(k_ref[...], s_ref[...], FIRST_BY_FIRST, preferred_element_type=F32) * SCALE


def prepare_kernel(q_hbm, g_hbm, o_hbm, q_ref, g_ref, delta_ref, o_ref, sems):
    rows = q_hbm.shape[0]
    flat, head_dim = q_ref.shape
    heads = flat // rows
    g_copies, o_copies, q_copies = (
        [
            pltpu.make_async_copy(
                source.at[:, h * head_dim : (h + 1) * head_dim],
                target.at[h * rows : (h + 1) * rows, :],
                sems.at[i, h],
            )
            for h in range(heads)
        ]
        for i, (source, target) in enumerate([(g_hbm, g_ref), (o_hbm, o_ref), (q_hbm, q_ref)])
    )
    for copy in g_copies + o_copies + q_copies:
        copy.start()
    for copy in g_copies + o_copies:
        copy.wait()
    for c in range(flat // 128):
        cs = slice(c * 128, (c + 1) * 128)
        product = g_ref[cs, :].astype(F32) * o_ref[cs, :].astype(F32)
        delta_ref[0:1, cs] = jnp.sum(product.T, axis=0, keepdims=True)
    for copy in q_copies:
        copy.wait()


def own_kernel(
    lens_ref, steps_ref, lse_ref, delta_ref, q_ref, g_ref, k_ref, v_ref,
    stats_ref, flags_ref, dk_ref, dv_ref, s_ref, w_ref,
):
    heads, rows = lse_ref.shape
    flat = heads * rows
    block = k_ref.shape[0]
    device = lax.axis_index(AXES)
    for h in range(heads):
        stats_ref[0:1, h * rows : (h + 1) * rows] = lse_ref[h : h + 1, :] * LOG2E
    stats_ref[1:2, :] = delta_ref[0:1, :]
    column = lax.broadcasted_iota(I32, (1, flat), 1)
    head = jnp.zeros((1, flat), I32)
    for h in range(1, heads):
        head = head + (column >= h * rows).astype(I32)
    local = column - head * rows + (block - rows)
    base = device * block
    query_pos = local + base

    def one_end(i, carry):
        end, starts, first = carry
        end = end + lens_ref[i]
        starts = jnp.where(query_pos >= end, end, starts)
        first = jnp.where(base + (block - rows) >= end, end, first)
        return end, starts, first

    zero = jnp.int32(0)
    _, starts, first = lax.fori_loop(
        0, lens_ref.shape[0], one_end, (zero, jnp.zeros((1, flat), I32), zero)
    )
    stats_ref[2:3, :] = (starts - base).astype(F32)
    stats_ref[3:4, :] = local.astype(F32)
    for t in range(steps_ref.shape[0]):
        owner = device - t
        active = (owner >= 0) & (steps_ref[t, device] == owner) & (first < (owner + 1) * block)
        flags_ref[t] = active.astype(I32)
    block_kernel(
        0, flags_ref, stats_ref, q_ref, g_ref, k_ref, v_ref, dk_ref, dv_ref, s_ref, w_ref
    )


def block_kernel(
    distance, flags_ref, stats_ref, q_ref, g_ref, k_ref, v_ref, dk_ref, dv_ref, s_ref, w_ref
):
    @pl.when(flags_ref[distance] == 1)
    def _():
        make_weights(distance, k_ref, v_ref, q_ref, g_ref, stats_ref, w_ref, s_ref)
        key_value_grads(q_ref, g_ref, w_ref, s_ref, dk_ref, dv_ref)

    @pl.when(flags_ref[distance] == 0)
    def _():
        dk_ref[...] = jnp.zeros_like(dk_ref)
        dv_ref[...] = jnp.zeros_like(dv_ref)


def queries_kernel(flags_ref, *refs):
    count = (len(refs) - 2) // 2
    k_refs, s_refs, (out_ref, dq_ref) = refs[:count], refs[count : 2 * count], refs[2 * count :]
    rows, width = out_ref.shape
    head_dim = k_refs[0].shape[1]
    dq_ref[...] = jnp.zeros_like(dq_ref)
    for t in range(count):

        @pl.when(flags_ref[t] == 1)
        def _(t=t):
            dq_ref[...] += query_grads(k_refs[t], s_refs[t])

    by_row = dq_ref[...].T
    for h in range(width // head_dim):
        out_ref[:, h * head_dim : (h + 1) * head_dim] = by_row[h * rows : (h + 1) * rows, :]


def call(kernel, name, outs, scratch, args, places=None, smem_outs=(), flops=0, limit=40 << 20):
    vmem, smem = pl.BlockSpec(memory_space=pltpu.VMEM), pl.BlockSpec(memory_space=pltpu.SMEM)
    if places is None:
        places = [smem] + [vmem] * (len(args) - 1)
    return pl.pallas_call(
        kernel,
        name=name,
        out_shape=[jax.ShapeDtypeStruct(s, d) for s, d in outs],
        in_specs=places,
        out_specs=[smem if i in smem_outs else vmem for i in range(len(outs))],
        scratch_shapes=scratch,
        cost_estimate=pl.CostEstimate(flops=flops, bytes_accessed=0, transcendentals=0),
        compiler_params=pltpu.CompilerParams(vmem_limit_bytes=limit),
    )(*args)


def local(queries, grad_out, attn_out, saved_lse, key_rows, value_rows, doc_lengths, read_steps):
    rows, width = queries.shape
    block, head_dim = key_rows.shape
    heads = width // head_dim
    flat = rows * heads
    half = ((block, head_dim), BF16)
    full = ((block, head_dim), F32)
    scores = ((block, flat), BF16)
    flat_rows = ((flat, head_dim), BF16)
    total = ((head_dim, flat), F32)
    k1 = passed_along(key_rows, 1)
    v3 = passed_along(value_rows, 3)
    vmem, smem, hbm = (
        pl.BlockSpec(memory_space=space) for space in (pltpu.VMEM, pltpu.SMEM, pltpu.HBM)
    )
    q, g, delta = call(
        prepare_kernel, "prepare",
        [flat_rows, flat_rows, ((8, flat), F32)],
        [pltpu.VMEM(*flat_rows), pltpu.SemaphoreType.DMA((3, heads))],
        (queries, grad_out, attn_out), [hbm] * 3, flops=20_000_000_000, limit=212 << 18,
    )

    def grads(distance, k, v, outs):
        return call(
            functools.partial(block_kernel, distance), f"block_{distance}",
            [*outs, scores], [pltpu.VMEM(*scores)], (flags, stats, q, g, k, v),
        )

    key_late, value_late, delta = lax.optimization_barrier((key_rows, value_rows, delta))
    v1 = passed_along(value_late, 1)
    k3 = passed_along(key_late, 3)
    stats, flags, dk0, dv0, s0 = call(
        own_kernel, "block_0",
        [((8, flat), F32), ((8,), I32), full, full, scores], [pltpu.VMEM(*scores)],
        (doc_lengths, read_steps.T, saved_lse, delta, q, g, key_rows, value_rows),
        [smem] * 2 + [vmem] * 6, smem_outs=(1,),
    )
    k1, s0_a = lax.optimization_barrier((k1, s0))
    v3, s0_b = lax.optimization_barrier((v3, s0))
    k2 = passed_along(k1, 1)
    v2 = passed_along(v3, -1)
    v1, s0 = lax.optimization_barrier((v1, s0))
    dk1, dv1, s1 = grads(1, k1, v1, [full, half])
    dv1r = passed_along(dv1, -1)
    k2, v2, k3, s1 = lax.optimization_barrier((k2, v2, k3, s1))
    dk2, dv2, s2 = grads(2, k2, v2, [half, half])
    dk2r = passed_along(dk2, -1)
    dv2r = passed_along(dv2, 1)
    k3, s2, dv1r = lax.optimization_barrier((k3, s2, dv1r))
    dk3, dv3, s3 = grads(3, k3, v3, [half, full])
    dk3r = passed_along(dk3, -3)
    dv2r, dk2r, flags = lax.optimization_barrier((dv2r, dk2r, flags))
    dv3 = (dv3 + dv2r.astype(F32)).astype(BF16)
    dk2r, dv3 = lax.optimization_barrier((dk2r, dv3))
    dv3r = passed_along(dv3, -3)
    dk1r = passed_along((dk1 + dk2r.astype(F32)).astype(BF16), -1)
    (grad_queries,) = call(
        queries_kernel, "queries",
        [((rows, width), F32)], [pltpu.VMEM(*total)],
        (flags, key_rows, k1, k2, k3, s0, s1, s2, s3),
    )
    grad_keys = dk0 + dk3r.astype(F32) + dk1r.astype(F32)
    grad_values = dv0 + dv1r.astype(F32) + dv3r.astype(F32)
    return grad_queries, grad_keys, grad_values


def solution(mesh):
    return jax.shard_map(
        local,
        mesh=mesh,
        in_specs=(
            P(AXES, None),
            P(AXES, None),
            P(AXES, None),
            P(None, AXES),
            P(AXES, None),
            P(AXES, None),
            P(),
            P(),
        ),
        out_specs=(P(AXES, None), P(AXES, None), P(AXES, None)),
        check_vma=False,
    )
```

```python
import functools

import jax
import jax.numpy as jnp
from jax import lax
from jax.experimental import pallas as pl
from jax.experimental.pallas import tpu as pltpu
from jax.sharding import PartitionSpec as P

AXES = ("cpx", "cpy")
HEAD_DIM = 128
SCALE = HEAD_DIM**-0.5
LOG2E = 1.4426950408889634
KEY_TILE = 128
ROW_TILE = 512
LAST_BY_LAST = (((1,), (1,)), ((), ()))
FIRST_BY_FIRST = (((0,), (0,)), ((), ()))
F32, BF16, I32 = jnp.float32, jnp.bfloat16, jnp.int32


def passed_along(value, steps):
    count = lax.axis_size(AXES)
    return lax.ppermute(value, AXES, [(d, (d + steps) % count) for d in range(count)])


def make_weights(distance, k_ref, v_ref, q_ref, g_ref, stats_ref, w_ref, s_ref):
    block, flat = w_ref.shape
    rows = flat // 8

    for j in range(flat // ROW_TILE):
        cs = slice(j * ROW_TILE, (j + 1) * ROW_TILE)
        q, g = q_ref[cs, :], g_ref[cs, :]
        lse, delta = stats_ref[0:1, cs], stats_ref[1:2, cs]
        first_key = stats_ref[2:3, cs] + float(distance * block)
        for i in range(block // KEY_TILE):
            ks = slice(i * KEY_TILE, (i + 1) * KEY_TILE)
            scores = lax.dot_general(k_ref[ks, :], q, LAST_BY_LAST, preferred_element_type=F32)
            grad_w = lax.dot_general(v_ref[ks, :], g, LAST_BY_LAST, preferred_element_type=F32)
            key = (lax.broadcasted_iota(I32, (KEY_TILE, ROW_TILE), 0) + i * KEY_TILE).astype(F32)
            allowed = key >= first_key
            if distance == 0 and (i + 1) * KEY_TILE > block - rows:
                allowed = allowed & (key <= stats_ref[3:4, cs])
            weights = jnp.where(allowed, jnp.exp2(scores * (SCALE * LOG2E) - lse), 0.0)
            w_ref[ks, cs] = weights.astype(BF16)
            s_ref[ks, cs] = (weights * (grad_w - delta)).astype(BF16)


def key_value_grads(q_ref, g_ref, w_ref, s_ref, dk_ref, dv_ref):
    dk = jnp.dot(s_ref[...], q_ref[...], preferred_element_type=F32) * SCALE
    dk_ref[...] = dk.astype(dk_ref.dtype)
    dv_ref[...] = jnp.dot(w_ref[...], g_ref[...], preferred_element_type=F32).astype(dv_ref.dtype)


def query_grads(k_ref, s_ref):
    return lax.dot_general(k_ref[...], s_ref[...], FIRST_BY_FIRST, preferred_element_type=F32) * SCALE


def prepare_kernel(q_hbm, g_hbm, o_hbm, q_ref, g_ref, delta_ref, o_ref, sems):
    rows = q_hbm.shape[0]
    flat, head_dim = q_ref.shape
    heads = flat // rows
    g_copies, o_copies, q_copies = (
        [
            pltpu.make_async_copy(
                source.at[:, h * head_dim : (h + 1) * head_dim],
                target.at[h * rows : (h + 1) * rows, :],
                sems.at[i, h],
            )
            for h in range(heads)
        ]
        for i, (source, target) in enumerate([(g_hbm, g_ref), (o_hbm, o_ref), (q_hbm, q_ref)])
    )
    for copy in g_copies + o_copies + q_copies:
        copy.start()
    for copy in g_copies + o_copies:
        copy.wait()
    for c in range(flat // 128):
        cs = slice(c * 128, (c + 1) * 128)
        product = g_ref[cs, :].astype(F32) * o_ref[cs, :].astype(F32)
        delta_ref[0:1, cs] = jnp.sum(product.T, axis=0, keepdims=True)
    for copy in q_copies:
        copy.wait()


def own_kernel(
    lens_ref, steps_ref, lse_ref, delta_ref, q_ref, g_ref, k_ref, v_ref,
    stats_ref, flags_ref, dk_ref, dv_ref, s_ref, w_ref,
):
    heads, rows = lse_ref.shape
    flat = heads * rows
    block = k_ref.shape[0]
    device = lax.axis_index(AXES)
    for h in range(heads):
        stats_ref[0:1, h * rows : (h + 1) * rows] = lse_ref[h : h + 1, :] * LOG2E
    stats_ref[1:2, :] = delta_ref[0:1, :]
    column = lax.broadcasted_iota(I32, (1, flat), 1)
    head = jnp.zeros((1, flat), I32)
    for h in range(1, heads):
        head = head + (column >= h * rows).astype(I32)
    local = column - head * rows + (block - rows)
    base = device * block
    query_pos = local + base

    def one_end(i, carry):
        end, starts, first = carry
        end = end + lens_ref[i]
        starts = jnp.where(query_pos >= end, end, starts)
        first = jnp.where(base + (block - rows) >= end, end, first)
        return end, starts, first

    zero = jnp.int32(0)
    _, starts, first = lax.fori_loop(
        0, lens_ref.shape[0], one_end, (zero, jnp.zeros((1, flat), I32), zero)
    )
    stats_ref[2:3, :] = (starts - base).astype(F32)
    stats_ref[3:4, :] = local.astype(F32)
    for t in range(steps_ref.shape[0]):
        owner = device - t
        active = (owner >= 0) & (steps_ref[t, device] == owner) & (first < (owner + 1) * block)
        flags_ref[t] = active.astype(I32)
    block_kernel(
        0, flags_ref, stats_ref, q_ref, g_ref, k_ref, v_ref, dk_ref, dv_ref, s_ref, w_ref
    )


def block_kernel(
    distance, flags_ref, stats_ref, q_ref, g_ref, k_ref, v_ref, dk_ref, dv_ref, s_ref, w_ref
):
    @pl.when(flags_ref[distance] == 1)
    def _():
        make_weights(distance, k_ref, v_ref, q_ref, g_ref, stats_ref, w_ref, s_ref)
        key_value_grads(q_ref, g_ref, w_ref, s_ref, dk_ref, dv_ref)

    @pl.when(flags_ref[distance] == 0)
    def _():
        dk_ref[...] = jnp.zeros_like(dk_ref)
        dv_ref[...] = jnp.zeros_like(dv_ref)


def queries_kernel(flags_ref, *refs):
    count = (len(refs) - 2) // 2
    k_refs, s_refs, (out_ref, dq_ref) = refs[:count], refs[count : 2 * count], refs[2 * count :]
    rows, width = out_ref.shape
    head_dim = k_refs[0].shape[1]
    dq_ref[...] = jnp.zeros_like(dq_ref)
    for t in range(count):

        @pl.when(flags_ref[t] == 1)
        def _(t=t):
            dq_ref[...] += query_grads(k_refs[t], s_refs[t])

    by_row = dq_ref[...].T
    for h in range(width // head_dim):
        out_ref[:, h * head_dim : (h + 1) * head_dim] = by_row[h * rows : (h + 1) * rows, :]


def call(kernel, name, outs, scratch, args, places=None, smem_outs=(), flops=0, limit=40 << 20):
    vmem, smem = pl.BlockSpec(memory_space=pltpu.VMEM), pl.BlockSpec(memory_space=pltpu.SMEM)
    if places is None:
        places = [smem] + [vmem] * (len(args) - 1)
    return pl.pallas_call(
        kernel,
        name=name,
        out_shape=[jax.ShapeDtypeStruct(s, d) for s, d in outs],
        in_specs=places,
        out_specs=[smem if i in smem_outs else vmem for i in range(len(outs))],
        scratch_shapes=scratch,
        cost_estimate=pl.CostEstimate(flops=flops, bytes_accessed=0, transcendentals=0),
        compiler_params=pltpu.CompilerParams(vmem_limit_bytes=limit),
    )(*args)


def local(queries, grad_out, attn_out, saved_lse, key_rows, value_rows, doc_lengths, read_steps):
    rows, width = queries.shape
    block, head_dim = key_rows.shape
    heads = width // head_dim
    flat = rows * heads
    half = ((block, head_dim), BF16)
    full = ((block, head_dim), F32)
    scores = ((block, flat), BF16)
    flat_rows = ((flat, head_dim), BF16)
    total = ((head_dim, flat), F32)
    k1 = passed_along(key_rows, 1)
    v3 = passed_along(value_rows, 3)
    vmem, smem, hbm = (
        pl.BlockSpec(memory_space=space) for space in (pltpu.VMEM, pltpu.SMEM, pltpu.HBM)
    )
    q, g, delta = call(
        prepare_kernel, "prepare",
        [flat_rows, flat_rows, ((8, flat), F32)],
        [pltpu.VMEM(*flat_rows), pltpu.SemaphoreType.DMA((3, heads))],
        (queries, grad_out, attn_out), [hbm] * 3, flops=20_000_000_000, limit=212 << 18,
    )

    def grads(distance, k, v, outs):
        return call(
            functools.partial(block_kernel, distance), f"block_{distance}",
            [*outs, scores], [pltpu.VMEM(*scores)], (flags, stats, q, g, k, v),
        )

    key_late, value_late, delta = lax.optimization_barrier((key_rows, value_rows, delta))
    v1 = passed_along(value_late, 1)
    k3 = passed_along(key_late, 3)
    stats, flags, dk0, dv0, s0 = call(
        own_kernel, "block_0",
        [((8, flat), F32), ((8,), I32), full, full, scores], [pltpu.VMEM(*scores)],
        (doc_lengths, read_steps.T, saved_lse, delta, q, g, key_rows, value_rows),
        [smem] * 2 + [vmem] * 6, smem_outs=(1,),
    )
    k1, v3, s0 = lax.optimization_barrier((k1, v3, s0))
    k2 = passed_along(k1, 1)
    v2 = passed_along(v3, -1)
    v1, k3, s0 = lax.optimization_barrier((v1, k3, s0))
    dk1, dv1, s1 = grads(1, k1, v1, [full, half])
    dv1r = passed_along(dv1, -1)
    k2, v2, s1 = lax.optimization_barrier((k2, v2, s1))
    dk2, dv2, s2 = grads(2, k2, v2, [half, half])
    dk2r = passed_along(dk2, -1)
    dv2r = passed_along(dv2, 1)
    k3, s2, dv1r = lax.optimization_barrier((k3, s2, dv1r))
    dk3, dv3, s3 = grads(3, k3, v3, [half, full])
    dk3r = passed_along(dk3, -3)
    dv2r, dk2r, flags = lax.optimization_barrier((dv2r, dk2r, flags))
    dv3 = (dv3 + dv2r.astype(F32)).astype(BF16)
    dk2r, dv3 = lax.optimization_barrier((dk2r, dv3))
    dv3r = passed_along(dv3, -3)
    dk1r = passed_along((dk1 + dk2r.astype(F32)).astype(BF16), -1)
    (grad_queries,) = call(
        queries_kernel, "queries",
        [((rows, width), F32)], [pltpu.VMEM(*total)],
        (flags, key_rows, k1, k2, k3, s0, s1, s2, s3),
    )
    grad_keys = dk0 + dk3r.astype(F32) + dk1r.astype(F32)
    grad_values = dv0 + dv1r.astype(F32) + dv3r.astype(F32)
    return grad_queries, grad_keys, grad_values


def solution(mesh):
    return jax.shard_map(
        local,
        mesh=mesh,
        in_specs=(
            P(AXES, None),
            P(AXES, None),
            P(AXES, None),
            P(None, AXES),
            P(AXES, None),
            P(AXES, None),
            P(),
            P(),
        ),
        out_specs=(P(AXES, None), P(AXES, None), P(AXES, None)),
        check_vma=False,
    )
```

```python
import functools

import jax
import jax.numpy as jnp
from jax import lax
from jax.experimental import pallas as pl
from jax.experimental.pallas import tpu as pltpu
from jax.sharding import PartitionSpec as P

AXES = ("cpx", "cpy")
HEAD_DIM = 128
SCALE = HEAD_DIM**-0.5
LOG2E = 1.4426950408889634
KEY_TILE = 128
ROW_TILE = 512
LAST_BY_LAST = (((1,), (1,)), ((), ()))
FIRST_BY_FIRST = (((0,), (0,)), ((), ()))
F32, BF16, I32 = jnp.float32, jnp.bfloat16, jnp.int32


def passed_along(value, steps):
    count = lax.axis_size(AXES)
    return lax.ppermute(value, AXES, [(d, (d + steps) % count) for d in range(count)])


def make_weights(distance, k_ref, v_ref, q_ref, g_ref, stats_ref, w_ref, s_ref):
    block, flat = w_ref.shape
    rows = flat // 8

    for j in range(flat // ROW_TILE):
        cs = slice(j * ROW_TILE, (j + 1) * ROW_TILE)
        q, g = q_ref[cs, :], g_ref[cs, :]
        lse, delta = stats_ref[0:1, cs], stats_ref[1:2, cs]
        first_key = stats_ref[2:3, cs] + float(distance * block)
        for i in range(block // KEY_TILE):
            ks = slice(i * KEY_TILE, (i + 1) * KEY_TILE)
            scores = lax.dot_general(k_ref[ks, :], q, LAST_BY_LAST, preferred_element_type=F32)
            grad_w = lax.dot_general(v_ref[ks, :], g, LAST_BY_LAST, preferred_element_type=F32)
            key = (lax.broadcasted_iota(I32, (KEY_TILE, ROW_TILE), 0) + i * KEY_TILE).astype(F32)
            allowed = key >= first_key
            if distance == 0 and (i + 1) * KEY_TILE > block - rows:
                allowed = allowed & (key <= stats_ref[3:4, cs])
            weights = jnp.where(allowed, jnp.exp2(scores * (SCALE * LOG2E) - lse), 0.0)
            w_ref[ks, cs] = weights.astype(BF16)
            s_ref[ks, cs] = (weights * (grad_w - delta)).astype(BF16)


def key_value_grads(q_ref, g_ref, w_ref, s_ref, dk_ref, dv_ref):
    dk = jnp.dot(s_ref[...], q_ref[...], preferred_element_type=F32) * SCALE
    dk_ref[...] = dk.astype(dk_ref.dtype)
    dv_ref[...] = jnp.dot(w_ref[...], g_ref[...], preferred_element_type=F32).astype(dv_ref.dtype)


def query_grads(k_ref, s_ref):
    return lax.dot_general(k_ref[...], s_ref[...], FIRST_BY_FIRST, preferred_element_type=F32) * SCALE


def prepare_kernel(q_hbm, g_hbm, o_hbm, q_ref, g_ref, delta_ref, o_ref, sems):
    rows = q_hbm.shape[0]
    flat, head_dim = q_ref.shape
    heads = flat // rows
    g_copies, o_copies, q_copies = (
        [
            pltpu.make_async_copy(
                source.at[:, h * head_dim : (h + 1) * head_dim],
                target.at[h * rows : (h + 1) * rows, :],
                sems.at[i, h],
            )
            for h in range(heads)
        ]
        for i, (source, target) in enumerate([(g_hbm, g_ref), (o_hbm, o_ref), (q_hbm, q_ref)])
    )
    for copy in g_copies + o_copies + q_copies:
        copy.start()
    for copy in g_copies + o_copies:
        copy.wait()
    for c in range(flat // 128):
        cs = slice(c * 128, (c + 1) * 128)
        product = g_ref[cs, :].astype(F32) * o_ref[cs, :].astype(F32)
        delta_ref[0:1, cs] = jnp.sum(product.T, axis=0, keepdims=True)
    for copy in q_copies:
        copy.wait()


def own_kernel(
    lens_ref, steps_ref, lse_ref, delta_ref, q_ref, g_ref, k_ref, v_ref,
    stats_ref, flags_ref, dk_ref, dv_ref, s_ref, w_ref,
):
    heads, rows = lse_ref.shape
    flat = heads * rows
    block = k_ref.shape[0]
    device = lax.axis_index(AXES)
    for h in range(heads):
        stats_ref[0:1, h * rows : (h + 1) * rows] = lse_ref[h : h + 1, :] * LOG2E
    stats_ref[1:2, :] = delta_ref[0:1, :]
    column = lax.broadcasted_iota(I32, (1, flat), 1)
    head = jnp.zeros((1, flat), I32)
    for h in range(1, heads):
        head = head + (column >= h * rows).astype(I32)
    local = column - head * rows + (block - rows)
    base = device * block
    query_pos = local + base

    def one_end(i, carry):
        end, starts, first = carry
        end = end + lens_ref[i]
        starts = jnp.where(query_pos >= end, end, starts)
        first = jnp.where(base + (block - rows) >= end, end, first)
        return end, starts, first

    zero = jnp.int32(0)
    _, starts, first = lax.fori_loop(
        0, lens_ref.shape[0], one_end, (zero, jnp.zeros((1, flat), I32), zero)
    )
    stats_ref[2:3, :] = (starts - base).astype(F32)
    stats_ref[3:4, :] = local.astype(F32)
    for t in range(steps_ref.shape[0]):
        owner = device - t
        active = (owner >= 0) & (steps_ref[t, device] == owner) & (first < (owner + 1) * block)
        flags_ref[t] = active.astype(I32)
    block_kernel(
        0, flags_ref, stats_ref, q_ref, g_ref, k_ref, v_ref, dk_ref, dv_ref, s_ref, w_ref
    )


def block_kernel(
    distance, flags_ref, stats_ref, q_ref, g_ref, k_ref, v_ref, dk_ref, dv_ref, s_ref, w_ref
):
    @pl.when(flags_ref[distance] == 1)
    def _():
        make_weights(distance, k_ref, v_ref, q_ref, g_ref, stats_ref, w_ref, s_ref)
        key_value_grads(q_ref, g_ref, w_ref, s_ref, dk_ref, dv_ref)

    @pl.when(flags_ref[distance] == 0)
    def _():
        dk_ref[...] = jnp.zeros_like(dk_ref)
        dv_ref[...] = jnp.zeros_like(dv_ref)


def queries_kernel(flags_ref, *refs):
    count = (len(refs) - 2) // 2
    k_refs, s_refs, (out_ref, dq_ref) = refs[:count], refs[count : 2 * count], refs[2 * count :]
    rows, width = out_ref.shape
    head_dim = k_refs[0].shape[1]
    dq_ref[...] = jnp.zeros_like(dq_ref)
    for t in range(count):

        @pl.when(flags_ref[t] == 1)
        def _(t=t):
            dq_ref[...] += query_grads(k_refs[t], s_refs[t])

    by_row = dq_ref[...].T
    for h in range(width // head_dim):
        out_ref[:, h * head_dim : (h + 1) * head_dim] = by_row[h * rows : (h + 1) * rows, :]


def call(kernel, name, outs, scratch, args, places=None, smem_outs=(), flops=0, limit=40 << 20):
    vmem, smem = pl.BlockSpec(memory_space=pltpu.VMEM), pl.BlockSpec(memory_space=pltpu.SMEM)
    if places is None:
        places = [smem] + [vmem] * (len(args) - 1)
    return pl.pallas_call(
        kernel,
        name=name,
        out_shape=[jax.ShapeDtypeStruct(s, d) for s, d in outs],
        in_specs=places,
        out_specs=[smem if i in smem_outs else vmem for i in range(len(outs))],
        scratch_shapes=scratch,
        cost_estimate=pl.CostEstimate(flops=flops, bytes_accessed=0, transcendentals=0),
        compiler_params=pltpu.CompilerParams(vmem_limit_bytes=limit),
    )(*args)


def local(queries, grad_out, attn_out, saved_lse, key_rows, value_rows, doc_lengths, read_steps):
    rows, width = queries.shape
    block, head_dim = key_rows.shape
    heads = width // head_dim
    flat = rows * heads
    half = ((block, head_dim), BF16)
    full = ((block, head_dim), F32)
    scores = ((block, flat), BF16)
    flat_rows = ((flat, head_dim), BF16)
    total = ((head_dim, flat), F32)
    k1 = passed_along(key_rows, 1)
    v3 = passed_along(value_rows, 3)
    vmem, smem, hbm = (
        pl.BlockSpec(memory_space=space) for space in (pltpu.VMEM, pltpu.SMEM, pltpu.HBM)
    )
    q, g, delta = call(
        prepare_kernel, "prepare",
        [flat_rows, flat_rows, ((8, flat), F32)],
        [pltpu.VMEM(*flat_rows), pltpu.SemaphoreType.DMA((3, heads))],
        (queries, grad_out, attn_out), [hbm] * 3, flops=20_000_000_000, limit=212 << 18,
    )

    def grads(distance, k, v, outs):
        return call(
            functools.partial(block_kernel, distance), f"block_{distance}",
            [*outs, scores], [pltpu.VMEM(*scores)], (flags, stats, q, g, k, v),
        )

    key_late, value_late, delta = lax.optimization_barrier((key_rows, value_rows, delta))
    v1 = passed_along(value_late, 1)
    k3 = passed_along(key_late, 3)
    stats, flags, dk0, dv0, s0 = call(
        own_kernel, "block_0",
        [((8, flat), F32), ((8,), I32), full, full, scores], [pltpu.VMEM(*scores)],
        (doc_lengths, read_steps.T, saved_lse, delta, q, g, key_rows, value_rows),
        [smem] * 2 + [vmem] * 6, smem_outs=(1,),
    )
    k1, s0_a = lax.optimization_barrier((k1, s0))
    v3, s0_b = lax.optimization_barrier((v3, s0))
    k2 = passed_along(k1, 1)
    v2 = passed_along(v3, -1)
    v1, k3, s0 = lax.optimization_barrier((v1, k3, s0))
    dk1, dv1, s1 = grads(1, k1, v1, [full, half])
    dv1r = passed_along(dv1, -1)
    k2, v2, s1 = lax.optimization_barrier((k2, v2, s1))
    dk2, dv2, s2 = grads(2, k2, v2, [half, half])
    dk2r = passed_along(dk2, -1)
    dv2r = passed_along(dv2, 1)
    k3, s2, dv1r = lax.optimization_barrier((k3, s2, dv1r))
    dk3, dv3, s3 = grads(3, k3, v3, [half, full])
    dk3r = passed_along(dk3, -3)
    dv2r, dk2r, flags = lax.optimization_barrier((dv2r, dk2r, flags))
    dv3 = (dv3 + dv2r.astype(F32)).astype(BF16)
    dk2r, dv3 = lax.optimization_barrier((dk2r, dv3))
    dv3r = passed_along(dv3, -3)
    dk1r = passed_along((dk1 + dk2r.astype(F32)).astype(BF16), -1)
    (grad_queries,) = call(
        queries_kernel, "queries",
        [((rows, width), F32)], [pltpu.VMEM(*total)],
        (flags, key_rows, k1, k2, k3, s0, s1, s2, s3),
    )
    grad_keys = dk0 + dk3r.astype(F32) + dk1r.astype(F32)
    grad_values = dv0 + dv1r.astype(F32) + dv3r.astype(F32)
    return grad_queries, grad_keys, grad_values


def solution(mesh):
    return jax.shard_map(
        local,
        mesh=mesh,
        in_specs=(
            P(AXES, None),
            P(AXES, None),
            P(AXES, None),
            P(None, AXES),
            P(AXES, None),
            P(AXES, None),
            P(),
            P(),
        ),
        out_specs=(P(AXES, None), P(AXES, None), P(AXES, None)),
        check_vma=False,
    )
```
